32 devices in a mesh: section: 2 (over core), group: 2 (over y), shard: 8 (over z, x).
Axes of the slice: x: 2, y: 2, z: 4, core: 2. Of those that a mesh axis runs over, the one named last changes fastest.
Arguments:
- cache: bfloat16 [2, 2, 8, 8, 128, 2048], P('section', 'group', None, 'shard'), may hold values from -4 to 4
- queries: bfloat16 [2, 2, 8, 4, 16384], P('section', 'group', None, None, 'shard'), may hold values from -19 to 19
- fresh_kv: bfloat16 [2, 2, 8, 4, 2048], P('section', 'group', None, None, 'shard'), may hold values from -4 to 4
- lengths: int32 [2, 2, 8], P('section', 'group'), may hold values from 2 to 1020, as said below
- targets: int32 [2, 8], P('group'), may hold values from 0 to 2, as said below
Outputs:
- attended: bfloat16 [2, 2, 8, 4, 16384], P('section', 'group', None, None, 'shard')
- handed: bfloat16 [2, 2, 2, 2, 8, 128, 2048], P('section', 'group', None, None, 'shard')
The draws below stay inside these ranges and needn't reach their ends.
Inputs may be any that keep to these rules, and one draw needn't show every extreme that they name: `lengths`: each row has at least two cached positions, and in every section and group some row has exactly 1020. `targets`: the value 2 means that the prompt is not handed this round; at most 2 rows of one prefill group name one decode group, and some decode group is named by exactly 2 rows of every prefill group.
All inputs are finite; a program needn't handle non-finite values.
Results may differ from the reference program's by a relative error of at most 0.0044.
Values may be sent and summed in bfloat16 or wider, within the bound.
A program may use at most 128 MiB of HBM per device.

```python
import math
import jax
import jax.numpy as jnp
from jax import lax

HQ = 128
KVH = 8
DH = 128
ROWS = 8
CTX_DEV = 128
STEPS = 4
CAP = 2
GROUPS = 2
CTX = 1024
N_SHARD = 8


def draw_cache(key, part):
    key = jax.random.fold_in(key, 1)
    shard_count = CTX // CTX_DEV
    shape = (2, GROUPS, ROWS, shard_count, CTX_DEV, 2 * KVH * DH)
    base_values = jnp.clip(jax.random.normal(key, shape, jnp.float32), -4.0, 4.0)
    return base_values.astype(jnp.bfloat16)


def draw_queries(key, part):
    key = jax.random.fold_in(key, 2)
    shape = (2, GROUPS, ROWS, STEPS, HQ * DH)
    base_values = jnp.clip(jax.random.normal(key, shape, jnp.float32), -4.0, 4.0)
    return base_values.astype(jnp.bfloat16)


def draw_lengths(key, part):
    key = jax.random.fold_in(key, 3)
    split_keys = jax.random.split(key, 2)
    longest = CTX - STEPS
    drawn = jax.random.randint(split_keys[0], (2, GROUPS, ROWS), 2, longest + 1)
    chosen_row = jax.random.randint(split_keys[1], (2, GROUPS, 1), 0, ROWS)
    row_ids = jnp.arange(ROWS, dtype=jnp.int32)[None, None, :]
    return jnp.where(row_ids == chosen_row, longest, drawn).astype(jnp.int32)


def draw_targets(key, part):
    key = jax.random.fold_in(key, 4)
    split_keys = jax.random.split(key, 3)
    row_order = jax.vmap(lambda single_key: jax.random.permutation(single_key, ROWS))(jax.random.split(split_keys[0], GROUPS))
    counts = jax.random.randint(split_keys[1], (GROUPS, GROUPS), 0, CAP + 1)
    busiest = jax.random.randint(split_keys[2], (), 0, GROUPS)
    counts = jnp.where(jnp.arange(GROUPS)[None, :] == busiest, CAP, counts)
    slot_ids = jnp.arange(GROUPS * CAP, dtype=jnp.int32)
    slot_target = slot_ids // CAP
    is_live = (slot_ids % CAP)[None, :] < counts[:, slot_target]
    slot_values = jnp.where(is_live, slot_target[None, :], GROUPS)
    targets = jnp.full((GROUPS, ROWS), GROUPS, jnp.int32)
    targets = targets.at[jnp.arange(GROUPS)[:, None], row_order[:, :GROUPS * CAP]].set(slot_values)
    return targets.astype(jnp.int32)


def shard_levels(rng, shape, cuts, least, top_value):
    def one(axis_at, parts):
        draws = jax.random.uniform(jax.random.fold_in(jax.random.fold_in(rng, 6), axis_at), (parts,), jnp.float32, least / len(cuts), top_value / len(cuts))
        return jnp.repeat(jnp.exp(draws), shape[axis_at] // parts).reshape((-1,) + (1,) * (len(shape) - axis_at - 1))

    factor_of = one(*cuts[0])
    for cut in cuts[1:]:
        factor_of = factor_of * one(*cut)
    return factor_of


def normal_values(rng, extent, deviation, bound, shards=(), held_as=jnp.bfloat16):
    factor_of = shard_levels(rng, extent, shards, -0.22, 0.18) if shards else 1.0
    values = jax.random.normal(rng, extent, jnp.float32) * deviation * factor_of
    return jnp.minimum(jnp.maximum(values, -bound), bound).astype(held_as)


def setup_inputs(seed: int = 0) -> dict:
    key_list = jax.random.split(jax.random.key(seed), 6)
    return {
        "cache": draw_cache(jax.random.fold_in(key_list[5], 71), 0),
        "queries": draw_queries(jax.random.fold_in(key_list[5], 71), 0),
        "fresh_kv": normal_values(key_list[2], (2, GROUPS, ROWS, STEPS, 2 * KVH * DH), 1.0, 4.0, ((0, 2), (1, 2), (4, 8))),
        "lengths": draw_lengths(jax.random.fold_in(key_list[5], 71), 0),
        "targets": draw_targets(jax.random.fold_in(key_list[5], 71), 0),
    }


NEGATIVE = -jnp.inf

def cache_positions(section_id):
    shard_ids = jnp.arange(N_SHARD, dtype=jnp.int32)[:, None]
    slot_ids = jnp.arange(CTX_DEV, dtype=jnp.int32)[None, :]
    return jnp.where(section_id == 0, shard_ids * CTX_DEV + slot_ids, slot_ids * N_SHARD + shard_ids).reshape(-1)

def attend_row(cache_row, query_row, fresh_row, row_length, section_id):
    key_width = KVH * DH
    group_size = HQ // KVH
    flattened = cache_row.reshape(CTX, 2 * key_width).astype(jnp.float32)
    cached_keys = flattened[:, :key_width].reshape(CTX, KVH, DH)
    cached_values = flattened[:, key_width:].reshape(CTX, KVH, DH)
    fresh_all = fresh_row.astype(jnp.float32)
    fresh_keys = fresh_all[:, :key_width].reshape(STEPS, KVH, DH)
    fresh_values = fresh_all[:, key_width:].reshape(STEPS, KVH, DH)
    query_heads = query_row.astype(jnp.float32).reshape(STEPS, KVH, group_size, DH)
    score_scale = 1.0 / math.sqrt(DH)
    highest = lax.Precision.HIGHEST
    cache_scores = jnp.einsum('sKgd,cKd->Kgsc', query_heads, cached_keys, precision=highest) * score_scale
    cache_scores = jnp.where(cache_positions(section_id) < row_length, cache_scores, NEGATIVE)
    fresh_scores = jnp.einsum('sKgd,tKd->Kgst', query_heads, fresh_keys, precision=highest) * score_scale
    step_ids = jnp.arange(STEPS, dtype=jnp.int32)
    causal = step_ids[None, :] <= step_ids[:, None]
    fresh_scores = jnp.where(causal, fresh_scores, NEGATIVE)
    peak_score = jnp.maximum(lax.optimization_barrier(jnp.max(cache_scores, axis=-1)), lax.optimization_barrier(jnp.max(fresh_scores, axis=-1)))[..., None]
    cache_weights = lax.optimization_barrier(jnp.exp(cache_scores - peak_score).astype(jnp.bfloat16)).astype(jnp.float32)
    fresh_weights = lax.optimization_barrier(jnp.exp(fresh_scores - peak_score).astype(jnp.bfloat16)).astype(jnp.float32)
    weight_total = lax.optimization_barrier(jnp.sum(cache_weights, axis=-1)) + lax.optimization_barrier(jnp.sum(fresh_weights, axis=-1))
    mixed = jnp.einsum('Kgsc,cKd->sKgd', cache_weights, cached_values, precision=highest)
    mixed = mixed + jnp.einsum('Kgst,tKd->sKgd', fresh_weights, fresh_values, precision=highest)
    result = mixed / jnp.transpose(weight_total, (2, 0, 1))[..., None]
    return result.reshape(STEPS, HQ * DH).astype(jnp.bfloat16)

def prompt_sequence(cache_row, fresh_row, row_length):
    sequence = cache_row.reshape(CTX, 2 * KVH * DH)
    offset = jnp.arange(CTX, dtype=jnp.int32) - row_length
    one_hot = (offset[:, None] == jnp.arange(STEPS, dtype=jnp.int32)[None, :]).astype(jnp.float32)
    written = jnp.dot(one_hot, fresh_row.astype(jnp.float32), precision=lax.Precision.HIGHEST)
    return jnp.where(offset[:, None] < 0, sequence.astype(jnp.float32), written).astype(jnp.bfloat16)

def release_group(cache_group, fresh_group, length_group, target_group):
    row_ids = jnp.arange(ROWS, dtype=jnp.int32)
    same_target = target_group[:, None] == target_group[None, :]
    target_rank = lax.optimization_barrier(jnp.sum(same_target & (row_ids[None, :] < row_ids[:, None]), axis=1)).astype(jnp.int32)
    slot_ids = jnp.arange(GROUPS * CAP, dtype=jnp.int32)
    matches = (target_group[None, :] == (slot_ids // CAP)[:, None]) & (target_rank[None, :] == (slot_ids % CAP)[:, None])
    present = jnp.any(matches, axis=1)
    source_row = jnp.argmax(matches.astype(jnp.int32), axis=1).astype(jnp.int32)

    def single(record):
        picked_row, is_live = record
        sequence = prompt_sequence(cache_group[picked_row], fresh_group[picked_row], length_group[picked_row])
        return jnp.where(is_live, sequence, jnp.zeros_like(sequence))
    return lax.map(single, (source_row, present))

def reference(cache, queries, fresh_kv, lengths, targets):
    kv_width = 2 * KVH * DH
    total_rows = 2 * GROUPS * ROWS
    section_ids = jnp.repeat(jnp.arange(2, dtype=jnp.int32), GROUPS * ROWS)

    def attend_record(record):
        return attend_row(*record)
    attended = lax.map(attend_record, (cache.reshape(total_rows, N_SHARD, CTX_DEV, kv_width), queries.reshape(total_rows, STEPS, HQ * DH), fresh_kv.reshape(total_rows, STEPS, kv_width), lengths.reshape(total_rows), section_ids))
    attended = attended.reshape(2, GROUPS, ROWS, STEPS, HQ * DH)
    released = jnp.stack([release_group(cache[0, group_id], fresh_kv[0, group_id], lengths[0, group_id], targets[group_id]) for group_id in range(GROUPS)])
    released = released.reshape(GROUPS, GROUPS, CAP, CTX, kv_width)
    sent_layout = released.reshape(GROUPS, GROUPS, CAP, N_SHARD, CTX_DEV, kv_width)
    kept_layout = jnp.transpose(released, (1, 0, 2, 3, 4)).reshape(GROUPS, GROUPS, CAP, CTX_DEV, N_SHARD, kv_width)
    kept_layout = jnp.transpose(kept_layout, (0, 1, 2, 4, 3, 5))
    handed = jnp.stack([sent_layout, kept_layout])
    return (attended, handed)
```

```python
import functools
import math

import jax
import jax.numpy as jnp
from jax import lax
from jax.experimental import pallas as pl
from jax.experimental.pallas import tpu as pltpu
from jax.sharding import PartitionSpec as P

HQ = 128
KVH = 8
DH = 128
CAP = 2
FAR = -1e30
MESH = pl.DeviceIdType.MESH
F32 = jnp.float32
BF16 = jnp.bfloat16


def kernel(
    dims,
    cache_ref,
    q_ref,
    fresh_ref,
    len_ref,
    tgt_ref,
    att_ref,
    handed_ref,
    cv,
    fg,
    ff,
    qg,
    part,
    got,
    stat,
    gstat,
    fac,
    rel,
    perm,
    load_sem,
    out_sem,
    fs,
    fr,
    qs,
    qr,
    ps,
    pr,
    ss,
    sr,
    hs,
    hr,
):
    n, groups, rows, steps, slots, width = dims
    me = lax.axis_index("shard")
    sec = lax.axis_index("section")
    grp = lax.axis_index("group")
    hc = HQ // n
    sg = steps * hc
    wb = width // n
    pp = slots // n
    scale = 1.0 / math.sqrt(DH)
    other = 1 - sec

    load = pltpu.make_async_copy(cache_ref, cv, load_sem)
    load.start()

    barrier = pltpu.get_barrier_semaphore()

    def greet_peer(i, c):
        pl.semaphore_signal(
            barrier, inc=1, device_id={"shard": lax.rem(me + i, n)}, device_id_type=MESH
        )
        return c

    def greet_other(i, c):
        pl.semaphore_signal(
            barrier,
            inc=1,
            device_id={"section": other, "group": i // n, "shard": i % n},
            device_id_type=MESH,
        )
        return c

    lax.fori_loop(1, n, greet_peer, 0)
    lax.fori_loop(0, groups * n, greet_other, 0)
    pl.semaphore_wait(barrier, n - 1 + groups * n)

    def fresh_copy(to, slot):
        return pltpu.make_async_remote_copy(
            fresh_ref, fg.at[slot], fs.at[to], fr.at[slot], {"shard": to}, MESH
        )

    def query_copy(to, slot):
        return pltpu.make_async_remote_copy(
            q_ref, qg.at[slot], qs.at[to], qr.at[slot], {"shard": to}, MESH
        )

    def part_copy(to, slot):
        return pltpu.make_async_remote_copy(
            part.at[to], got.at[slot], ps.at[to], pr.at[slot], {"shard": to}, MESH
        )

    def stat_copy(to, slot):
        return pltpu.make_async_remote_copy(
            stat.at[to], gstat.at[slot], ss.at[to], sr.at[slot], {"shard": to}, MESH
        )

    def hand_copy(grp_to, shard_to, slot_grp, slot_shard):
        return pltpu.make_async_remote_copy(
            perm.at[grp_to, shard_to],
            handed_ref.at[slot_grp, :, slot_shard],
            hs.at[grp_to * n + shard_to],
            hr.at[slot_grp * n + slot_shard],
            {"section": 1, "group": grp_to, "shard": shard_to},
            MESH,
        )

    def send_fresh(i, c):
        fresh_copy(lax.rem(me + i, n), me).start()
        return c

    def send_query(i, c):
        query_copy(lax.rem(me + i, n), me).start()
        return c

    lax.fori_loop(1, n, send_fresh, 0)
    lax.fori_loop(1, n, send_query, 0)

    fg[me] = fresh_ref[...]
    qg[me] = q_ref[...]

    def wait_fresh(i, c):
        fresh_copy(me, lax.rem(me + n - i, n)).wait_recv()
        return c

    lax.fori_loop(1, n, wait_fresh, 0)
    per = max(1, 128 // wb)
    for j in range(0, n, per):
        pieces = [fg[j + i].astype(F32) for i in range(per)]
        piece = pieces[0] if per == 1 else jnp.concatenate(pieces, axis=1)
        for r in range(rows):
            ff[r, :, j * wb : (j + per) * wb] = piece[r * steps : (r + 1) * steps]
    load.wait()

    slot_rows = lax.broadcasted_iota(jnp.int32, (slots, 128), 0)
    place_rows = jnp.where(sec == 0, me * slots + slot_rows, slot_rows * n + me)

    def insert(r, c):
        off = place_rows - len_ref[r]
        keep = (off < 0).astype(F32).astype(BF16)
        hot = [(off == t).astype(F32).astype(BF16) for t in range(steps)]
        lines = ff[r]
        for w in range(width // 128):
            cols = slice(w * 128, (w + 1) * 128)
            y = cv[r, :, cols] * keep
            for t in range(steps):
                line = jnp.broadcast_to(lines[t : t + 1, cols], (slots, 128)).astype(BF16)
                y = y + hot[t] * line
            cv[r, :, cols] = y
        return c

    lax.fori_loop(0, rows, insert, 0)

    @pl.when(sec == 0)
    def _():
        q_ids = lax.broadcasted_iota(jnp.int32, (slots, slots), 0)
        i_ids = lax.broadcasted_iota(jnp.int32, (slots, slots), 1)
        order = ((q_ids % pp) * n + q_ids // pp == i_ids).astype(F32)
        tgt = [tgt_ref[r] for r in range(rows)]
        tile = 512
        for d in range(groups):
            count = jnp.int32(0)
            src = [jnp.int32(0)] * CAP
            for r in range(rows):
                hit = tgt[r] == d
                for k in range(CAP):
                    src[k] = jnp.where(hit & (count == k), r, src[k])
                count = count + hit.astype(jnp.int32)
            for k in range(CAP):
                live = (count > k).astype(F32)
                mover = (order * live).astype(BF16)
                for w in range(0, width, tile):
                    x = cv[src[k], :, w : w + tile]
                    y = (x.astype(F32) * live).reshape(n, pp, tile).astype(BF16)
                    rel[d, k, :, :, w : w + tile] = y
                    z = jnp.dot(mover, x, preferred_element_type=F32)
                    perm[d, :, k, :, w : w + tile] = z.reshape(n, pp, tile).astype(BF16)
        pltpu.make_async_copy(rel, handed_ref, out_sem).start()

        def send_hand(i, c):
            to = lax.rem(me + i, n)
            for d in range(groups):
                dst_group = lax.rem(grp + d, groups)
                hand_copy(dst_group, to, grp, me).start()
            return c

        lax.fori_loop(0, n, send_hand, 0)

    lane = lax.broadcasted_iota(jnp.int32, (sg, slots), 1)
    sub = lax.broadcasted_iota(jnp.int32, (sg, slots), 0)
    place = jnp.where(sec == 0, me * slots + lane, lane * n + me) - sub // hc
    stat_lane = lax.broadcasted_iota(jnp.int32, (sg, 128), 1)

    def attend(i, c):
        j = lax.rem(me + n - i, n)

        @pl.when(i > 0)
        def _():
            query_copy(me, j).wait_recv()

        kv = (j * hc) // (HQ // KVH)
        k_cols = pl.ds(pl.multiple_of(kv * DH, DH), DH)
        v_cols = pl.ds(pl.multiple_of((KVH + kv) * DH, DH), DH)
        lse_all = jnp.zeros((sg, 128), F32)
        for r in range(rows):
            s = lax.dot_general(
                qg[j, r],
                cv[r, :, k_cols],
                (((1,), (1,)), ((), ())),
                preferred_element_type=F32,
            )
            s = jnp.where(place <= len_ref[r], s * scale, FAR)
            m = jnp.max(s, axis=1, keepdims=True)
            p = jnp.exp(s - m).astype(BF16)
            total = jnp.sum(p.astype(F32), axis=1, keepdims=True)
            o = jnp.dot(p, cv[r, :, v_cols], preferred_element_type=F32)
            part[j, r] = (o / total).astype(BF16)
            lse_all = jnp.where(stat_lane == r, m + jnp.log(total), lse_all)
        stat[j] = lse_all

        @pl.when(i > 0)
        def _():
            stat_copy(j, me).start()
            part_copy(j, me).start()

        return c

    lax.fori_loop(0, n, attend, 0)
    gstat[me] = stat[me]
    got[me] = part[me]

    def wait_stat(i, c):
        stat_copy(me, lax.rem(me + i, n)).wait_recv()
        return c

    lax.fori_loop(1, n, wait_stat, 0)
    peak = gstat[0]
    for j in range(1, n):
        peak = jnp.maximum(peak, gstat[j])
    total = jnp.zeros_like(peak)
    for j in range(n):
        e = jnp.exp(gstat[j] - peak)
        fac[j] = e
        total = total + e
    inverse = 1.0 / total

    def wait_part(i, c):
        part_copy(me, lax.rem(me + i, n)).wait_recv()
        return c

    lax.fori_loop(1, n, wait_part, 0)
    for r in range(rows):
        acc = jnp.zeros((sg, DH), F32)
        for j in range(n):
            acc = acc + got[j, r].astype(F32) * fac[j, :, r : r + 1]
        att_ref[r] = (acc * inverse[:, r : r + 1]).astype(BF16)

    def wait_sends(i, c):
        to = lax.rem(me + i, n)
        fresh_copy(to, me).wait_send()
        query_copy(to, me).wait_send()
        stat_copy(to, me).wait_send()
        part_copy(to, me).wait_send()
        return c

    lax.fori_loop(1, n, wait_sends, 0)

    @pl.when(sec == 0)
    def _():
        def wait_hand(i, c):
            hand_copy(i // n, i % n, grp, me).wait_send()
            return c

        lax.fori_loop(0, groups * n, wait_hand, 0)
        pltpu.make_async_copy(rel, handed_ref, out_sem).wait()

    @pl.when(sec == 1)
    def _():
        def wait_hand(i, c):
            hand_copy(grp, me, i // n, i % n).wait_recv()
            return c

        lax.fori_loop(0, groups * n, wait_hand, 0)


def on_device(n, groups, cache, queries, fresh_kv, lengths, targets):
    rows, slots, width = cache.shape[2], cache.shape[4], cache.shape[5]
    steps = queries.shape[3]
    hc = HQ // n
    sg = steps * hc
    wb = width // n
    pp = slots // n
    dims = (n, groups, rows, steps, slots, width)
    vmem = pl.BlockSpec(memory_space=pltpu.VMEM)
    smem = pl.BlockSpec(memory_space=pltpu.SMEM)
    hbm = pl.BlockSpec(memory_space=pl.ANY)
    dma = pltpu.SemaphoreType.DMA
    attended, handed = pl.pallas_call(
        functools.partial(kernel, dims),
        out_shape=(
            jax.ShapeDtypeStruct((rows, sg, DH), BF16),
            jax.ShapeDtypeStruct((groups, CAP, n, pp, width), BF16),
        ),
        in_specs=[hbm, vmem, vmem, smem, smem],
        out_specs=(vmem, hbm),
        scratch_shapes=[
            pltpu.VMEM((rows, slots, width), BF16),
            pltpu.VMEM((n, rows * steps, wb), BF16),
            pltpu.VMEM((rows, steps, width), F32),
            pltpu.VMEM((n, rows, sg, DH), BF16),
            pltpu.VMEM((n, rows, sg, DH), BF16),
            pltpu.VMEM((n, rows, sg, DH), BF16),
            pltpu.VMEM((n, sg, 128), F32),
            pltpu.VMEM((n, sg, 128), F32),
            pltpu.VMEM((n, sg, 128), F32),
            pltpu.VMEM((groups, CAP, n, pp, width), BF16),
            pltpu.VMEM((groups, n, CAP, pp, width), BF16),
            dma,
            dma,
            dma((n,)),
            dma((n,)),
            dma((n,)),
            dma((n,)),
            dma((n,)),
            dma((n,)),
            dma((n,)),
            dma((n,)),
            dma((groups * n,)),
            dma((groups * n,)),
        ],
        compiler_params=pltpu.CompilerParams(
            collective_id=0, has_side_effects=True, vmem_limit_bytes=56 * 1024 * 1024
        ),
    )(
        cache.reshape(rows, slots, width),
        queries.reshape(rows, sg, DH),
        fresh_kv.reshape(rows * steps, wb),
        lengths.reshape(rows),
        targets.reshape(rows),
    )
    return (
        attended.reshape(1, 1, rows, steps, hc * DH),
        handed.reshape(1, 1, groups, CAP, 1, slots, width),
    )


def solution(mesh):
    in_specs = (
        P("section", "group", None, "shard", None, None),
        P("section", "group", None, None, "shard"),
        P("section", "group", None, None, "shard"),
        P("section", "group", None),
        P("group", None),
    )
    out_specs = (
        P("section", "group", None, None, "shard"),
        P("section", "group", None, None, "shard", None, None),
    )
    return jax.shard_map(
        functools.partial(on_device, mesh.shape["shard"], mesh.shape["group"]),
        mesh=mesh,
        in_specs=in_specs,
        out_specs=out_specs,
        check_vma=False,
    )
```

```python
import functools
import math

import jax
import jax.numpy as jnp
from jax import lax
from jax.experimental import pallas as pl
from jax.experimental.pallas import tpu as pltpu
from jax.sharding import PartitionSpec as P

HQ = 128
KVH = 8
DH = 128
CAP = 2
FAR = -1e30
MESH = pl.DeviceIdType.MESH
F32 = jnp.float32
BF16 = jnp.bfloat16


def kernel(
    dims,
    cache_ref,
    q_ref,
    fresh_ref,
    len_ref,
    tgt_ref,
    att_ref,
    handed_ref,
    cv,
    fg,
    ff,
    qg,
    part,
    got,
    stat,
    gstat,
    part2,
    got2,
    stat2,
    gstat2,
    rel,
    perm,
    load_sem,
    out_sem,
    fs,
    fr,
    qs,
    qdown,
    qx,
    qr,
    ps,
    pr,
    ss,
    sr,
    ps2,
    pr2,
    ss2,
    sr2,
    hs,
    hr,
):
    n, groups, rows, steps, slots, width = dims
    nx = side(n)
    nz = n // nx
    me = lax.axis_index("shard")
    sec = lax.axis_index("section")
    grp = lax.axis_index("group")
    z = me // nx
    x = lax.rem(me, nx)
    hc = HQ // n
    sg = steps * hc
    wb = width // n
    pp = slots // n
    scale = 1.0 / math.sqrt(DH)
    other = 1 - sec

    load = pltpu.make_async_copy(cache_ref, cv, load_sem)
    load.start()

    barrier = pltpu.get_barrier_semaphore()

    def greet_peer(i, c):
        pl.semaphore_signal(
            barrier, inc=1, device_id={"shard": lax.rem(me + i, n)}, device_id_type=MESH
        )
        return c

    def greet_other(i, c):
        pl.semaphore_signal(
            barrier,
            inc=1,
            device_id={"section": other, "group": i // n, "shard": i % n},
            device_id_type=MESH,
        )
        return c

    lax.fori_loop(1, n, greet_peer, 0)
    lax.fori_loop(0, groups * n, greet_other, 0)

    for r in range(rows):
        line = q_ref[r].astype(F32)
        qg[me, r] = jnp.concatenate(
            [line[:, g * DH : (g + 1) * DH] for g in range(hc)], axis=0
        ).astype(BF16)

    pl.semaphore_wait(barrier, n - 1 + groups * n)

    def fresh_copy(to, slot):
        return pltpu.make_async_remote_copy(
            fresh_ref, fg.at[slot], fs.at[to], fr.at[slot], {"shard": to}, MESH
        )

    def query_copy(slot, to, sem):
        return pltpu.make_async_remote_copy(
            qg.at[slot], qg.at[slot], sem, qr.at[slot], {"shard": to}, MESH
        )

    def across(i):
        return z * nx + lax.rem(x + i, nx)

    def part_copy(to_x, block, src_x):
        return pltpu.make_async_remote_copy(
            part.at[to_x * nz + block],
            got.at[src_x * nz + block],
            ps.at[to_x * nz + block],
            pr.at[src_x * nz + block],
            {"shard": z * nx + to_x},
            MESH,
        )

    def stat_copy(to_x, block, src_x):
        return pltpu.make_async_remote_copy(
            stat.at[to_x * nz + block],
            gstat.at[src_x * nz + block],
            ss.at[to_x * nz + block],
            sr.at[src_x * nz + block],
            {"shard": z * nx + to_x},
            MESH,
        )

    def part2_copy(to_z, src_z):
        return pltpu.make_async_remote_copy(
            part2.at[to_z],
            got2.at[src_z],
            ps2.at[to_z],
            pr2.at[src_z],
            {"shard": to_z * nx + x},
            MESH,
        )

    def stat2_copy(to_z, src_z):
        return pltpu.make_async_remote_copy(
            stat2.at[to_z],
            gstat2.at[src_z],
            ss2.at[to_z],
            sr2.at[src_z],
            {"shard": to_z * nx + x},
            MESH,
        )

    def hand_copy(grp_to, shard_to, slot_grp, slot_shard):
        return pltpu.make_async_remote_copy(
            perm.at[grp_to, shard_to],
            handed_ref.at[slot_grp, :, slot_shard],
            hs.at[grp_to * n + shard_to],
            hr.at[slot_grp * n + slot_shard],
            {"section": 1, "group": grp_to, "shard": shard_to},
            MESH,
        )

    def send_fresh(i, c):
        fresh_copy(lax.rem(me + i, n), me).start()
        return c

    lax.fori_loop(1, n, send_fresh, 0)

    def up(slot):
        return query_copy(slot, me + nx, qs.at[slot])

    def down(slot):
        return query_copy(slot, me - nx, qs.at[slot])

    def own_down():
        return query_copy(me, me - nx, qdown)

    def sideways(slot, i):
        return query_copy(slot, across(i), qx.at[(slot // nx) * nx + i])

    @pl.when(z < nz - 1)
    def _():
        up(me).start()

    @pl.when(z > 0)
    def _():
        own_down().start()

    for i in range(1, nx):
        sideways(me, i).start()

    def pass_on(d):
        low = me - d * nx
        high = me + d * nx

        @pl.when(z >= d)
        def _():
            query_copy(low, me, qr.at[low]).wait_recv()
            for i in range(1, nx):
                sideways(low, i).start()

            @pl.when(z < nz - 1)
            def _():
                up(low).start()

        @pl.when(z + d < nz)
        def _():
            query_copy(high, me, qr.at[high]).wait_recv()
            for i in range(1, nx):
                sideways(high, i).start()

            @pl.when(z > 0)
            def _():
                down(high).start()

    fg[me] = fresh_ref[...]

    def wait_fresh(i, c):
        fresh_copy(me, lax.rem(me + n - i, n)).wait_recv()
        return c

    lax.fori_loop(1, n, wait_fresh, 0)
    pass_on(1)
    per = max(1, 128 // wb)
    for j in range(0, n, per):
        pieces = [fg[j + i].astype(F32) for i in range(per)]
        ff[:, :, j * wb : (j + per) * wb] = (
            pieces[0] if per == 1 else jnp.concatenate(pieces, axis=2)
        )
    load.wait()

    slot_rows = lax.broadcasted_iota(jnp.int32, (slots, 128), 0)
    place_rows = jnp.where(sec == 0, me * slots + slot_rows, slot_rows * n + me)

    def insert(r, c):
        off = place_rows - len_ref[r]
        keep = (off < 0).astype(F32).astype(BF16)
        hot = [(off == t).astype(F32).astype(BF16) for t in range(steps)]
        lines = ff[r]
        for w in range(width // 128):
            cols = slice(w * 128, (w + 1) * 128)
            y = cv[r, :, cols] * keep
            for t in range(steps):
                line = jnp.broadcast_to(lines[t : t + 1, cols], (slots, 128)).astype(BF16)
                y = y + hot[t] * line
            cv[r, :, cols] = y
        return c

    lax.fori_loop(0, rows, insert, 0)
    if nz > 2:
        pass_on(2)

    @pl.when(sec == 0)
    def _():
        q_ids = lax.broadcasted_iota(jnp.int32, (slots, slots), 0)
        i_ids = lax.broadcasted_iota(jnp.int32, (slots, slots), 1)
        order = ((q_ids % pp) * n + q_ids // pp == i_ids).astype(F32)
        tgt = [tgt_ref[r] for r in range(rows)]
        tile = 512
        for d in range(groups):
            count = jnp.int32(0)
            src = [jnp.int32(0)] * CAP
            for r in range(rows):
                hit = tgt[r] == d
                for k in range(CAP):
                    src[k] = jnp.where(hit & (count == k), r, src[k])
                count = count + hit.astype(jnp.int32)
            for k in range(CAP):
                live = (count > k).astype(F32)
                mover = (order * live).astype(BF16)
                for w in range(0, width, tile):
                    y = cv[src[k], :, w : w + tile]
                    v = (y.astype(F32) * live).reshape(n, pp, tile).astype(BF16)
                    rel[d, k, :, :, w : w + tile] = v
                    v = jnp.dot(mover, y, preferred_element_type=F32)
                    perm[d, :, k, :, w : w + tile] = v.reshape(n, pp, tile).astype(BF16)
        pltpu.make_async_copy(rel, handed_ref, out_sem).start()

        def send_hand(i, c):
            to = lax.rem(me + i, n)
            for d in range(groups):
                hand_copy(lax.rem(grp + d, groups), to, grp, me).start()
            return c

        lax.fori_loop(0, n, send_hand, 0)

    for d in range(3, nz):
        pass_on(d)

    lane = lax.broadcasted_iota(jnp.int32, (sg, slots), 1)
    sub = lax.broadcasted_iota(jnp.int32, (sg, slots), 0)
    place = jnp.where(sec == 0, me * slots + lane, lane * n + me) - sub % steps
    stat_lane = lax.broadcasted_iota(jnp.int32, (sg, 128), 1)
    ones = jnp.ones((slots, DH), BF16)
    batch = 4

    def attend(j, row_list):
        kv = (j * hc) // (HQ // KVH)
        k_cols = pl.ds(pl.multiple_of(kv * DH, DH), DH)
        v_cols = pl.ds(pl.multiple_of((KVH + kv) * DH, DH), DH)
        scores = [
            lax.dot_general(
                qg[j, r],
                cv[r, :, k_cols],
                (((1,), (1,)), ((), ())),
                preferred_element_type=F32,
            )
            for r in row_list
        ]
        scores = [
            jnp.where(place <= len_ref[r], s * scale, FAR) for r, s in zip(row_list, scores)
        ]
        peaks = [jnp.max(s, axis=1, keepdims=True) for s in scores]
        weights = [jnp.exp(s - m).astype(BF16) for s, m in zip(scores, peaks)]
        mixed = [
            jnp.dot(
                p,
                jnp.concatenate([cv[r, :, v_cols], ones], axis=1),
                preferred_element_type=F32,
            )
            for r, p in zip(row_list, weights)
        ]
        out = []
        for m, o in zip(peaks, mixed):
            total = o[:, DH:]
            out.append((o[:, :DH] / total, m + jnp.log(total)))
        return out

    def first(i, c):
        to_x = lax.rem(x + 1 + i // nz, nx)
        block = lax.rem(z + i, nz)
        j = block * nx + to_x
        query_copy(j, me, qr.at[j]).wait_recv()
        slot = to_x * nz + block
        lse_all = jnp.zeros((sg, 128), F32)
        for r0 in range(0, rows, batch):
            row_list = list(range(r0, r0 + batch))
            for r, (o, lse) in zip(row_list, attend(j, row_list)):
                part[slot, r] = o.astype(BF16)
                lse_all = jnp.where(stat_lane == r, lse, lse_all)
        stat[slot] = jnp.transpose(lse_all)[:rows]
        stat_copy(to_x, block, x).start()
        part_copy(to_x, block, x).start()
        return c

    lax.fori_loop(0, (nx - 1) * nz, first, 0)

    def second(i, c):
        block = lax.rem(z + 1 + i, nz)
        j = block * nx + x
        for k in range(1, nx):
            src_x = lax.rem(x + k, nx)
            stat_copy(src_x, block, src_x).wait_recv()
            part_copy(src_x, block, src_x).wait_recv()
        theirs = [
            jnp.transpose(gstat[lax.rem(x + k, nx) * nz + block]) for k in range(1, nx)
        ]
        lse_all = jnp.zeros((sg, 128), F32)
        for r0 in range(0, rows, batch):
            row_list = list(range(r0, r0 + batch))
            for r, (o, lse) in zip(row_list, attend(j, row_list)):
                far = [jnp.broadcast_to(t[:, r : r + 1], (sg, DH)) for t in theirs]
                peak = functools.reduce(jnp.maximum, far, lse)
                e = jnp.exp(lse - peak)
                acc = o * e
                total = e
                for k in range(1, nx):
                    e = jnp.exp(far[k - 1] - peak)
                    slot = lax.rem(x + k, nx) * nz + block
                    acc = acc + got[slot, r].astype(F32) * e
                    total = total + e
                part2[block, r] = (acc / total).astype(BF16)
                lse_all = jnp.where(stat_lane == r, peak + jnp.log(total), lse_all)
        stat2[block] = jnp.transpose(lse_all)[:rows]

        @pl.when(i < nz - 1)
        def _():
            stat2_copy(block, z).start()
            part2_copy(block, z).start()

        return c

    lax.fori_loop(0, nz, second, 0)
    gstat2[z] = stat2[z]
    got2[z] = part2[z]

    def wait_stat(i, c):
        from_z = lax.rem(z + i, nz)
        stat2_copy(from_z, from_z).wait_recv()
        return c

    lax.fori_loop(1, nz, wait_stat, 0)
    peak = functools.reduce(jnp.maximum, [gstat2[j] for j in range(nz)])
    es = [jnp.exp(gstat2[j] - peak) for j in range(nz)]
    inverse = 1.0 / sum(es[1:], es[0])
    fac = [jnp.transpose(e * inverse) for e in es]

    def wait_part(i, c):
        from_z = lax.rem(z + i, nz)
        part2_copy(from_z, from_z).wait_recv()
        return c

    lax.fori_loop(1, nz, wait_part, 0)
    for r in range(rows):
        acc = jnp.zeros((sg, DH), F32)
        for j in range(nz):
            acc = acc + got2[j, r].astype(F32) * fac[j][:, r : r + 1]
        for g in range(hc):
            att_ref[r, :, g * DH : (g + 1) * DH] = acc[g * steps : (g + 1) * steps].astype(BF16)

    def wait_fresh_sends(i, c):
        fresh_copy(lax.rem(me + i, n), me).wait_send()
        return c

    lax.fori_loop(1, n, wait_fresh_sends, 0)

    @pl.when(z < nz - 1)
    def _():
        up(me).wait_send()

    @pl.when(z > 0)
    def _():
        own_down().wait_send()

    def wait_queries(block, c):
        slot = block * nx + x
        for i in range(1, nx):
            sideways(slot, i).wait_send()

        @pl.when((block < z) & (z < nz - 1))
        def _():
            up(slot).wait_send()

        @pl.when((block > z) & (z > 0))
        def _():
            down(slot).wait_send()

        return c

    lax.fori_loop(0, nz, wait_queries, 0)

    def wait_parts(i, c):
        to_x = lax.rem(x + 1 + i // nz, nx)
        stat_copy(to_x, lax.rem(z + i, nz), x).wait_send()
        part_copy(to_x, lax.rem(z + i, nz), x).wait_send()
        return c

    lax.fori_loop(0, (nx - 1) * nz, wait_parts, 0)

    def wait_parts2(i, c):
        stat2_copy(lax.rem(z + i, nz), z).wait_send()
        part2_copy(lax.rem(z + i, nz), z).wait_send()
        return c

    lax.fori_loop(1, nz, wait_parts2, 0)

    @pl.when(sec == 0)
    def _():
        def wait_hand(i, c):
            hand_copy(i // n, i % n, grp, me).wait_send()
            return c

        lax.fori_loop(0, groups * n, wait_hand, 0)
        pltpu.make_async_copy(rel, handed_ref, out_sem).wait()

    @pl.when(sec == 1)
    def _():
        def wait_hand(i, c):
            hand_copy(grp, me, i // n, i % n).wait_recv()
            return c

        lax.fori_loop(0, groups * n, wait_hand, 0)


def side(n):
    nx = max(1, math.isqrt(n // 2))
    while n % nx:
        nx -= 1
    return nx


def on_device(n, groups, cache, queries, fresh_kv, lengths, targets):
    rows, slots, width = cache.shape[2], cache.shape[4], cache.shape[5]
    steps = queries.shape[3]
    hc = HQ // n
    sg = steps * hc
    wb = width // n
    pp = slots // n
    nz = n // side(n)
    dims = (n, groups, rows, steps, slots, width)
    vmem = pl.BlockSpec(memory_space=pltpu.VMEM)
    smem = pl.BlockSpec(memory_space=pltpu.SMEM)
    hbm = pl.BlockSpec(memory_space=pl.ANY)
    dma = pltpu.SemaphoreType.DMA
    attended, handed = pl.pallas_call(
        functools.partial(kernel, dims),
        out_shape=(
            jax.ShapeDtypeStruct((rows, steps, hc * DH), BF16),
            jax.ShapeDtypeStruct((groups, CAP, n, pp, width), BF16),
        ),
        in_specs=[hbm, vmem, vmem, smem, smem],
        out_specs=(vmem, hbm),
        scratch_shapes=[
            pltpu.VMEM((rows, slots, width), BF16),
            pltpu.VMEM((n, rows, steps, wb), BF16),
            pltpu.VMEM((rows, steps, width), F32),
            pltpu.VMEM((n, rows, sg, DH), BF16),
            pltpu.VMEM((n, rows, sg, DH), BF16),
            pltpu.VMEM((n, rows, sg, DH), BF16),
            pltpu.VMEM((n, rows, sg), F32),
            pltpu.VMEM((n, rows, sg), F32),
            pltpu.VMEM((nz, rows, sg, DH), BF16),
            pltpu.VMEM((nz, rows, sg, DH), BF16),
            pltpu.VMEM((nz, rows, sg), F32),
            pltpu.VMEM((nz, rows, sg), F32),
            pltpu.VMEM((groups, CAP, n, pp, width), BF16),
            pltpu.VMEM((groups, n, CAP, pp, width), BF16),
            dma,
            dma,
            dma((n,)),
            dma((n,)),
            dma((n,)),
            dma,
            dma((n,)),
            dma((n,)),
            dma((n,)),
            dma((n,)),
            dma((n,)),
            dma((n,)),
            dma((nz,)),
            dma((nz,)),
            dma((nz,)),
            dma((nz,)),
            dma((groups * n,)),
            dma((groups * n,)),
        ],
        compiler_params=pltpu.CompilerParams(
            collective_id=0, has_side_effects=True, vmem_limit_bytes=56 * 1024 * 1024
        ),
    )(
        cache.reshape(rows, slots, width),
        queries.reshape(rows, steps, hc * DH),
        fresh_kv.reshape(rows, steps, wb),
        lengths.reshape(rows),
        targets.reshape(rows),
    )
    return (
        attended.reshape(1, 1, rows, steps, hc * DH),
        handed.reshape(1, 1, groups, CAP, 1, slots, width),
    )


def solution(mesh):
    in_specs = (
        P("section", "group", None, "shard", None, None),
        P("section", "group", None, None, "shard"),
        P("section", "group", None, None, "shard"),
        P("section", "group", None),
        P("group", None),
    )
    out_specs = (
        P("section", "group", None, None, "shard"),
        P("section", "group", None, None, "shard", None, None),
    )
    return jax.shard_map(
        functools.partial(on_device, mesh.shape["shard"], mesh.shape["group"]),
        mesh=mesh,
        in_specs=in_specs,
        out_specs=out_specs,
        check_vma=False,
    )
```

```python
import functools
import math

import jax
import jax.numpy as jnp
from jax import lax
from jax.experimental import pallas as pl
from jax.experimental.pallas import tpu as pltpu
from jax.sharding import PartitionSpec as P

HQ = 128
KVH = 8
DH = 128
CAP = 2
FAR = -1e30
MESH = pl.DeviceIdType.MESH
F32 = jnp.float32
BF16 = jnp.bfloat16


def kernel(
    dims,
    cache_ref,
    q_ref,
    fresh_ref,
    len_ref,
    tgt_ref,
    att_ref,
    handed_ref,
    cv,
    fg,
    ff,
    qg,
    part,
    got,
    stat,
    gstat,
    part2,
    got2,
    stat2,
    gstat2,
    rel,
    perm,
    load_sem,
    out_sem,
    fs,
    fr,
    qs,
    qdown,
    qx,
    qr,
    ps,
    pr,
    ss,
    sr,
    ps2,
    pr2,
    ss2,
    sr2,
    hs,
    hr,
):
    n, groups, rows, steps, slots, width = dims
    nx = side(n)
    nz = n // nx
    me = lax.axis_index("shard")
    sec = lax.axis_index("section")
    grp = lax.axis_index("group")
    z = me // nx
    x = lax.rem(me, nx)
    hc = HQ // n
    sg = steps * hc
    wb = width // n
    pp = slots // n
    scale = 1.0 / math.sqrt(DH)
    other = 1 - sec

    load = pltpu.make_async_copy(cache_ref, cv, load_sem)
    load.start()

    barrier = pltpu.get_barrier_semaphore()

    def greet_peer(i, c):
        pl.semaphore_signal(
            barrier, inc=1, device_id={"shard": lax.rem(me + i, n)}, device_id_type=MESH
        )
        return c

    def greet_other(i, c):
        pl.semaphore_signal(
            barrier,
            inc=1,
            device_id={"section": other, "group": i // n, "shard": i % n},
            device_id_type=MESH,
        )
        return c

    lax.fori_loop(1, n, greet_peer, 0)
    lax.fori_loop(0, groups * n, greet_other, 0)

    for r in range(rows):
        line = q_ref[r].astype(F32)
        qg[me, r] = jnp.concatenate(
            [line[:, g * DH : (g + 1) * DH] for g in range(hc)], axis=0
        ).astype(BF16)

    pl.semaphore_wait(barrier, n - 1 + groups * n)

    def fresh_copy(to, slot):
        return pltpu.make_async_remote_copy(
            fresh_ref, fg.at[slot], fs.at[to], fr.at[slot], {"shard": to}, MESH
        )

    def query_copy(slot, to, sem):
        return pltpu.make_async_remote_copy(
            qg.at[slot], qg.at[slot], sem, qr.at[slot], {"shard": to}, MESH
        )

    def across(i):
        return z * nx + lax.rem(x + i, nx)

    def part_copy(to_x, block, src_x):
        return pltpu.make_async_remote_copy(
            part.at[to_x * nz + block],
            got.at[src_x * nz + block],
            ps.at[to_x * nz + block],
            pr.at[src_x * nz + block],
            {"shard": z * nx + to_x},
            MESH,
        )

    def stat_copy(to_x, block, src_x):
        return pltpu.make_async_remote_copy(
            stat.at[to_x * nz + block],
            gstat.at[src_x * nz + block],
            ss.at[to_x * nz + block],
            sr.at[src_x * nz + block],
            {"shard": z * nx + to_x},
            MESH,
        )

    def part2_copy(to_z, src_z):
        return pltpu.make_async_remote_copy(
            part2.at[to_z],
            got2.at[src_z],
            ps2.at[to_z],
            pr2.at[src_z],
            {"shard": to_z * nx + x},
            MESH,
        )

    def stat2_copy(to_z, src_z):
        return pltpu.make_async_remote_copy(
            stat2.at[to_z],
            gstat2.at[src_z],
            ss2.at[to_z],
            sr2.at[src_z],
            {"shard": to_z * nx + x},
            MESH,
        )

    def hand_copy(grp_to, shard_to, slot_grp, slot_shard):
        return pltpu.make_async_remote_copy(
            perm.at[grp_to, shard_to],
            handed_ref.at[slot_grp, :, slot_shard],
            hs.at[grp_to * n + shard_to],
            hr.at[slot_grp * n + slot_shard],
            {"section": 1, "group": grp_to, "shard": shard_to},
            MESH,
        )

    def send_fresh(i, c):
        fresh_copy(lax.rem(me + i, n), me).start()
        return c

    lax.fori_loop(1, n, send_fresh, 0)

    def up(slot):
        return query_copy(slot, me + nx, qs.at[slot])

    def down(slot):
        return query_copy(slot, me - nx, qs.at[slot])

    def own_down():
        return query_copy(me, me - nx, qdown)

    def sideways(slot, i):
        return query_copy(slot, across(i), qx.at[(slot // nx) * nx + i])

    @pl.when(z < nz - 1)
    def _():
        up(me).start()

    @pl.when(z > 0)
    def _():
        own_down().start()

    for i in range(1, nx):
        sideways(me, i).start()

    def pass_on(d):
        low = me - d * nx
        high = me + d * nx

        @pl.when(z >= d)
        def _():
            query_copy(low, me, qr.at[low]).wait_recv()
            for i in range(1, nx):
                sideways(low, i).start()

            @pl.when(z < nz - 1)
            def _():
                up(low).start()

        @pl.when(z + d < nz)
        def _():
            query_copy(high, me, qr.at[high]).wait_recv()
            for i in range(1, nx):
                sideways(high, i).start()

            @pl.when(z > 0)
            def _():
                down(high).start()

    fg[me] = fresh_ref[...]

    def wait_fresh(i, c):
        fresh_copy(me, lax.rem(me + n - i, n)).wait_recv()
        return c

    lax.fori_loop(1, n, wait_fresh, 0)
    pass_on(1)
    per = max(1, 128 // wb)
    for j in range(0, n, per):
        pieces = [fg[j + i].astype(F32) for i in range(per)]
        ff[:, :, j * wb : (j + per) * wb] = (
            pieces[0] if per == 1 else jnp.concatenate(pieces, axis=2)
        )
    load.wait()

    def pick(d):
        count = jnp.int32(0)
        src = [jnp.int32(0)] * CAP
        for r in range(rows):
            hit = tgt_ref[r] == d
            for k in range(CAP):
                src[k] = jnp.where(hit & (count == k), r, src[k])
            count = count + hit.astype(jnp.int32)
        return src, [count > k for k in range(CAP)]

    @pl.when(sec == 0)
    def _():
        q_ids = lax.broadcasted_iota(jnp.int32, (slots, slots), 0)
        i_ids = lax.broadcasted_iota(jnp.int32, (slots, slots), 1)
        order = (q_ids % pp) * n + q_ids // pp == i_ids
        tile = 512
        ids = lax.broadcasted_iota(jnp.int32, (slots, tile), 0)
        at = me * slots + (ids % pp) * n + ids // pp
        for d in range(groups):
            src, lives = pick(d)
            for k in range(CAP):
                size = jnp.where(lives[k], len_ref[src[k]], -steps)
                mover = (order & (me * slots + i_ids < size)).astype(F32).astype(BF16)
                hot = [(at == size + t).astype(F32) for t in range(steps)]
                lines = ff[src[k]]
                for w in range(0, width, tile):
                    v = jnp.dot(mover, cv[src[k], :, w : w + tile], preferred_element_type=F32)
                    for t in range(steps):
                        v = v + hot[t] * lines[t : t + 1, w : w + tile]
                    perm[d, :, k, :, w : w + tile] = v.reshape(n, pp, tile).astype(BF16)

            def send_hand(i, c):
                hand_copy(d, lax.rem(me + i, n), grp, me).start()
                return c

            lax.fori_loop(0, n, send_hand, 0)


    slot_rows = lax.broadcasted_iota(jnp.int32, (slots, 128), 0)
    place_rows = jnp.where(sec == 0, me * slots + slot_rows, slot_rows * n + me)

    def insert(r, c):
        off = place_rows - len_ref[r]
        keep = (off < 0).astype(F32).astype(BF16)
        hot = [(off == t).astype(F32).astype(BF16) for t in range(steps)]
        lines = ff[r]
        for w in range(width // 128):
            cols = slice(w * 128, (w + 1) * 128)
            y = cv[r, :, cols] * keep
            for t in range(steps):
                line = jnp.broadcast_to(lines[t : t + 1, cols], (slots, 128)).astype(BF16)
                y = y + hot[t] * line
            cv[r, :, cols] = y
        return c

    lax.fori_loop(0, rows, insert, 0)
    for d in range(2, nz):
        pass_on(d)
    @pl.when(sec == 0)
    def _():
        tile = 512
        for d in range(groups):
            src, lives = pick(d)
            for k in range(CAP):
                live = lives[k].astype(F32)
                for w in range(0, width, tile):
                    y = cv[src[k], :, w : w + tile].astype(F32) * live
                    rel[d, k, :, :, w : w + tile] = y.reshape(n, pp, tile).astype(BF16)
        pltpu.make_async_copy(rel, handed_ref, out_sem).start()

    lane = lax.broadcasted_iota(jnp.int32, (sg, slots), 1)
    sub = lax.broadcasted_iota(jnp.int32, (sg, slots), 0)
    place = jnp.where(sec == 0, me * slots + lane, lane * n + me) - sub % steps
    stat_lane = lax.broadcasted_iota(jnp.int32, (sg, 128), 1)
    ones = jnp.ones((slots, DH), BF16)
    batch = 4

    def attend(j, row_list):
        kv = (j * hc) // (HQ // KVH)
        k_cols = pl.ds(pl.multiple_of(kv * DH, DH), DH)
        v_cols = pl.ds(pl.multiple_of((KVH + kv) * DH, DH), DH)
        scores = [
            lax.dot_general(
                qg[j, r],
                cv[r, :, k_cols],
                (((1,), (1,)), ((), ())),
                preferred_element_type=F32,
            )
            for r in row_list
        ]
        scores = [
            jnp.where(place <= len_ref[r], s * scale, FAR) for r, s in zip(row_list, scores)
        ]
        peaks = [jnp.max(s, axis=1, keepdims=True) for s in scores]
        weights = [jnp.exp(s - m).astype(BF16) for s, m in zip(scores, peaks)]
        mixed = [
            jnp.dot(
                p,
                jnp.concatenate([cv[r, :, v_cols], ones], axis=1),
                preferred_element_type=F32,
            )
            for r, p in zip(row_list, weights)
        ]
        out = []
        for m, o in zip(peaks, mixed):
            total = o[:, DH:]
            out.append((o[:, :DH] / total, m + jnp.log(total)))
        return out

    below = z
    above = nz - 1 - z

    def near(i):
        step = (i + 1) // 2
        inner = jnp.where(lax.rem(i, 2) == 1, z + step, z - step)
        outer = jnp.where(above > below, i, nz - 1 - i)
        return jnp.where(i <= 2 * jnp.minimum(below, above), inner, outer)

    def first(block, k, c):
        to_x = lax.rem(x + k, nx)
        j = block * nx + to_x
        query_copy(j, me, qr.at[j]).wait_recv()
        slot = to_x * nz + block
        lse_all = jnp.zeros((sg, 128), F32)
        for r0 in range(0, rows, batch):
            row_list = list(range(r0, r0 + batch))
            for r, (o, lse) in zip(row_list, attend(j, row_list)):
                part[slot, r] = o.astype(BF16)
                lse_all = jnp.where(stat_lane == r, lse, lse_all)
        stat[slot] = jnp.transpose(lse_all)[:rows]
        stat_copy(to_x, block, x).start()
        part_copy(to_x, block, x).start()
        return c

    def second(block):
        j = block * nx + x
        for k in range(1, nx):
            src_x = lax.rem(x + k, nx)
            stat_copy(src_x, block, src_x).wait_recv()
            part_copy(src_x, block, src_x).wait_recv()
        theirs = [
            jnp.transpose(gstat[lax.rem(x + k, nx) * nz + block]) for k in range(1, nx)
        ]
        lse_all = jnp.zeros((sg, 128), F32)
        for r0 in range(0, rows, batch):
            row_list = list(range(r0, r0 + batch))
            for r, (o, lse) in zip(row_list, attend(j, row_list)):
                far = [jnp.broadcast_to(t[:, r : r + 1], (sg, DH)) for t in theirs]
                peak = functools.reduce(jnp.maximum, far, lse)
                e = jnp.exp(lse - peak)
                acc = o * e
                total = e
                for k in range(1, nx):
                    e = jnp.exp(far[k - 1] - peak)
                    slot = lax.rem(x + k, nx) * nz + block
                    acc = acc + got[slot, r].astype(F32) * e
                    total = total + e
                part2[block, r] = (acc / total).astype(BF16)
                lse_all = jnp.where(stat_lane == r, peak + jnp.log(total), lse_all)
        stat2[block] = jnp.transpose(lse_all)[:rows]

        @pl.when(block != z)
        def _():
            stat2_copy(block, z).start()
            part2_copy(block, z).start()

    def turn(t, c):
        @pl.when(t < nz)
        def _():
            lax.fori_loop(1, nx, functools.partial(first, near(t)), 0)

        @pl.when(t >= 2)
        def _():
            second(jnp.where(t <= nz, near(t - 1), z))

        return c

    def turn_a(t, c):
        lax.fori_loop(1, nx, functools.partial(first, lax.rem(z + t, nz)), 0)
        return c

    def turn_b(t, c):
        second(lax.rem(z + 1 + t, nz))
        return c

    lax.fori_loop(0, nz, turn_a, 0)
    lax.fori_loop(0, nz, turn_b, 0)
    gstat2[z] = stat2[z]
    got2[z] = part2[z]

    def wait_stat(i, c):
        from_z = lax.rem(z + i, nz)
        stat2_copy(from_z, from_z).wait_recv()
        return c

    lax.fori_loop(1, nz, wait_stat, 0)
    peak = functools.reduce(jnp.maximum, [gstat2[j] for j in range(nz)])
    es = [jnp.exp(gstat2[j] - peak) for j in range(nz)]
    inverse = 1.0 / sum(es[1:], es[0])
    fac = [jnp.transpose(e * inverse) for e in es]

    def wait_part(i, c):
        from_z = lax.rem(z + i, nz)
        part2_copy(from_z, from_z).wait_recv()
        return c

    lax.fori_loop(1, nz, wait_part, 0)
    for r in range(rows):
        acc = jnp.zeros((sg, DH), F32)
        for j in range(nz):
            acc = acc + got2[j, r].astype(F32) * fac[j][:, r : r + 1]
        for g in range(hc):
            att_ref[r, :, g * DH : (g + 1) * DH] = acc[g * steps : (g + 1) * steps].astype(BF16)

    def wait_fresh_sends(i, c):
        fresh_copy(lax.rem(me + i, n), me).wait_send()
        return c

    lax.fori_loop(1, n, wait_fresh_sends, 0)

    @pl.when(z < nz - 1)
    def _():
        up(me).wait_send()

    @pl.when(z > 0)
    def _():
        own_down().wait_send()

    def wait_queries(block, c):
        slot = block * nx + x
        for i in range(1, nx):
            sideways(slot, i).wait_send()

        @pl.when((block < z) & (z < nz - 1))
        def _():
            up(slot).wait_send()

        @pl.when((block > z) & (z > 0))
        def _():
            down(slot).wait_send()

        return c

    lax.fori_loop(0, nz, wait_queries, 0)

    def wait_parts(i, c):
        to_x = lax.rem(x + 1 + i // nz, nx)
        stat_copy(to_x, lax.rem(z + i, nz), x).wait_send()
        part_copy(to_x, lax.rem(z + i, nz), x).wait_send()
        return c

    lax.fori_loop(0, (nx - 1) * nz, wait_parts, 0)

    def wait_parts2(i, c):
        stat2_copy(lax.rem(z + i, nz), z).wait_send()
        part2_copy(lax.rem(z + i, nz), z).wait_send()
        return c

    lax.fori_loop(1, nz, wait_parts2, 0)

    @pl.when(sec == 0)
    def _():
        def wait_hand(i, c):
            hand_copy(i // n, i % n, grp, me).wait_send()
            return c

        lax.fori_loop(0, groups * n, wait_hand, 0)
        pltpu.make_async_copy(rel, handed_ref, out_sem).wait()

    @pl.when(sec == 1)
    def _():
        def wait_hand(i, c):
            hand_copy(grp, me, i // n, i % n).wait_recv()
            return c

        lax.fori_loop(0, groups * n, wait_hand, 0)


def side(n):
    nx = max(1, math.isqrt(n // 2))
    while n % nx:
        nx -= 1
    return nx


def on_device(n, groups, cache, queries, fresh_kv, lengths, targets):
    rows, slots, width = cache.shape[2], cache.shape[4], cache.shape[5]
    steps = queries.shape[3]
    hc = HQ // n
    sg = steps * hc
    wb = width // n
    pp = slots // n
    nz = n // side(n)
    dims = (n, groups, rows, steps, slots, width)
    vmem = pl.BlockSpec(memory_space=pltpu.VMEM)
    smem = pl.BlockSpec(memory_space=pltpu.SMEM)
    hbm = pl.BlockSpec(memory_space=pl.ANY)
    dma = pltpu.SemaphoreType.DMA
    attended, handed = pl.pallas_call(
        functools.partial(kernel, dims),
        out_shape=(
            jax.ShapeDtypeStruct((rows, steps, hc * DH), BF16),
            jax.ShapeDtypeStruct((groups, CAP, n, pp, width), BF16),
        ),
        in_specs=[hbm, vmem, vmem, smem, smem],
        out_specs=(vmem, hbm),
        scratch_shapes=[
            pltpu.VMEM((rows, slots, width), BF16),
            pltpu.VMEM((n, rows, steps, wb), BF16),
            pltpu.VMEM((rows, steps, width), F32),
            pltpu.VMEM((n, rows, sg, DH), BF16),
            pltpu.VMEM((n, rows, sg, DH), BF16),
            pltpu.VMEM((n, rows, sg, DH), BF16),
            pltpu.VMEM((n, rows, sg), F32),
            pltpu.VMEM((n, rows, sg), F32),
            pltpu.VMEM((nz, rows, sg, DH), BF16),
            pltpu.VMEM((nz, rows, sg, DH), BF16),
            pltpu.VMEM((nz, rows, sg), F32),
            pltpu.VMEM((nz, rows, sg), F32),
            pltpu.VMEM((groups, CAP, n, pp, width), BF16),
            pltpu.VMEM((groups, n, CAP, pp, width), BF16),
            dma,
            dma,
            dma((n,)),
            dma((n,)),
            dma((n,)),
            dma,
            dma((n,)),
            dma((n,)),
            dma((n,)),
            dma((n,)),
            dma((n,)),
            dma((n,)),
            dma((nz,)),
            dma((nz,)),
            dma((nz,)),
            dma((nz,)),
            dma((groups * n,)),
            dma((groups * n,)),
        ],
        compiler_params=pltpu.CompilerParams(
            collective_id=0, has_side_effects=True, vmem_limit_bytes=56 * 1024 * 1024
        ),
    )(
        cache.reshape(rows, slots, width),
        queries.reshape(rows, steps, hc * DH),
        fresh_kv.reshape(rows, steps, wb),
        lengths.reshape(rows),
        targets.reshape(rows),
    )
    return (
        attended.reshape(1, 1, rows, steps, hc * DH),
        handed.reshape(1, 1, groups, CAP, 1, slots, width),
    )


def solution(mesh):
    in_specs = (
        P("section", "group", None, "shard", None, None),
        P("section", "group", None, None, "shard"),
        P("section", "group", None, None, "shard"),
        P("section", "group", None),
        P("group", None),
    )
    out_specs = (
        P("section", "group", None, None, "shard"),
        P("section", "group", None, None, "shard", None, None),
    )
    return jax.shard_map(
        functools.partial(on_device, mesh.shape["shard"], mesh.shape["group"]),
        mesh=mesh,
        in_specs=in_specs,
        out_specs=out_specs,
        check_vma=False,
    )
```
